256 devices in a mesh: sample: 16 (over x_lo, z), feat: 16 (over x_hi, y, core).
Axes of the slice: x: 4 (x_hi: 2, x_lo: 2; x = x_hi * 2 + x_lo), y: 4, z: 8, core: 2. Of those that a mesh axis runs over, the one named last changes fastest.
Arguments:
- features: bfloat16 [16384, 8192], P('sample', 'feat'), may hold values from -6 to 6
- panel: bfloat16 [8192, 1024], P('feat'), may hold values from -0.0625 to 0.0625
Outputs:
- update: float32 [8192, 1024], P('feat')
The draws below stay inside these ranges and needn't reach their ends.
All inputs are finite; a program needn't handle non-finite values.
Results may differ from the reference program's by a relative error of at most 0.0028.
Values may be sent and summed in bfloat16 or wider, within the bound.
A program may use at most 64 MiB of HBM per device.

```python
import math
import jax
import jax.numpy as jnp
from jax import lax

D = 8192
K = 1024
SAMPLES = 16384


def level_of(stream_key, extent, split, low, largest):
    gain = 1.0
    for axis_at, blocks in split:
        steps = jax.random.uniform(jax.random.fold_in(jax.random.fold_in(stream_key, 6), axis_at), (blocks,), jnp.float32, low / len(split), largest / len(split))
        gain = gain * jnp.repeat(jnp.exp(steps), extent[axis_at] // blocks).reshape((-1,) + (1,) * (len(extent) - 1 - axis_at))
    return gain


def bell_draw(own_key, dims, width, reach, shards=(), dtype=jnp.bfloat16):
    result = jax.random.normal(own_key, dims, jnp.float32) * width
    if len(shards) > 0:
        result = level_of(own_key, dims, shards, -0.22, 0.18) * result
    return jnp.clip(result, min=-reach, max=reach).astype(dtype)


def setup_inputs(seed: int = 0) -> dict:
    keys = jax.random.split(jax.random.key(seed), 3)
    return {
        "features": bell_draw(keys[0], (SAMPLES, D), 1.0, 6.0, ((0, 16), (1, 16))),
        "panel": bell_draw(keys[1], (D, K), D ** -0.5, 0.0625, ((0, 16),)),
    }


def reference(features, panel):
    total = features.shape[0]
    projected = jnp.dot(features, panel, preferred_element_type=jnp.float32).astype(jnp.bfloat16)
    gram = jnp.dot(projected.T, projected, preferred_element_type=jnp.float32) / total
    cross = jnp.dot(features.T, projected, preferred_element_type=jnp.float32) / total
    upper = jnp.triu(gram)
    upper_high = lax.optimization_barrier(upper.astype(jnp.bfloat16))
    upper_low = (upper - upper_high.astype(jnp.float32)).astype(jnp.bfloat16)
    penalty = jnp.dot(panel, upper_high, preferred_element_type=jnp.float32) + jnp.dot(panel, upper_low, preferred_element_type=jnp.float32)
    return (cross - penalty) * math.sqrt(D)
```

```python
import math

import jax
import jax.numpy as jnp
from jax import lax
from jax.experimental import pallas as pl
from jax.experimental.pallas import tpu as pltpu
from jax.sharding import PartitionSpec as P

MESH = pl.DeviceIdType.MESH
F32, BF16 = jnp.float32, jnp.bfloat16
D = 8192
CHUNKS = 4
SKEW = 3
PER_CHUNK = 40
BLK = 32


def dot(a, b):
    return jnp.dot(a, b, preferred_element_type=F32)


def kernel(scale, f_hbm, v_hbm, out_hbm, fv, ft, fx, vv, vx, psum, l1, t2, l2, t3, l3, proj, projt, wf,
           hop1, hop1r, hop2, hop2r, hop4, hop4r, xs, xr, ob, send_sem, recv_sem, local_sem):
    s, f = lax.axis_index("sample"), lax.axis_index("feat")
    xl, z = s // 8, s % 8
    xh, y, core = f // 8, (f // 2) % 4, f % 2
    q = y // 2
    p = (y + q) % 2
    half = fv.shape[0] // 2
    width = fv.shape[1]
    cw = vv.shape[1] // CHUNKS

    def feat_dev(xh_, y_, core_):
        return (s, xh_ * 8 + y_ * 2 + core_)

    def sample_dev(xl_, z_):
        return (xl_ * 8 + z_, f)

    y_a = y + 1 - 2 * (y % 2)
    y_b = 3 - y
    sib = feat_dev(xh, y, 1 - core)
    dev_a, dev_b = feat_dev(xh, y_a, core), feat_dev(xh, y_b, core)
    dev_x = feat_dev(1 - xh, y, core)
    up, down = sample_dev(xl, (z + 1) % 8), sample_dev(xl, (z + 7) % 8)
    dev_l = sample_dev(1 - xl, z)

    loads = []
    loads.append(pltpu.make_async_copy(f_hbm, fv, local_sem.at[0]))
    loads.append(pltpu.make_async_copy(v_hbm, vv, local_sem.at[1]))
    for load in loads:
        load.start()

    barrier = pltpu.get_barrier_semaphore()
    for partner in (sib, dev_a, dev_b, dev_x, up, down, dev_l):
        pl.semaphore_signal(barrier, inc=1, device_id=partner, device_id_type=MESH)
    pl.semaphore_wait(barrier, 7)

    sent = []

    def send(index, src, dst, device):
        copy = pltpu.make_async_remote_copy(
            src_ref=src, dst_ref=dst, send_sem=send_sem.at[index], recv_sem=recv_sem.at[index],
            device_id=device, device_id_type=MESH,
        )
        copy.start()
        sent.append(copy)
        return copy

    base = CHUNKS * PER_CHUNK
    got_f = send(base, f_hbm.at[pl.ds(pl.multiple_of((1 - core) * half, half), half), :], fx, sib)
    got_v = [
        send(base + 1 + c, v_hbm.at[:, c * cw:(c + 1) * cw], vx.at[c], sib) for c in range(CHUNKS)
    ]
    state = {}

    def project(c):
        if c == 0:
            for load in loads:
                load.wait()
            got_f.wait_recv()
        got_v[c].wait_recv()
        own = fv[pl.ds(pl.multiple_of(core * half, half), half), :]
        total = dot(own, vv[:, c * cw:(c + 1) * cw]) + dot(fx[...], vx[c])
        psum[c] = total.reshape(16, BLK, cw)
        i = c * PER_CHUNK
        state[c, "a1"] = send(i, psum.at[c, pl.ds((1 - p) * 4, 4)], l1.at[c, 0], dev_a)
        state[c, "b1"] = send(i + 1, psum.at[c, pl.ds(8 + (1 - q) * 4, 4)], l1.at[c, 1], dev_b)
        if c == 0:
            ft[...] = fv[...].T

    def halve2(c):
        i = c * PER_CHUNK + 2
        state[c, "a1"].wait_recv()
        t2[c, 0] = psum[c, pl.ds(p * 4, 4)] + l1[c, 0]
        state[c, "a2"] = send(i, t2.at[c, 0, pl.ds((1 - q) * 2, 2)], l2.at[c, 0], dev_b)
        state[c, "b1"].wait_recv()
        t2[c, 1] = psum[c, pl.ds(8 + q * 4, 4)] + l1[c, 1]
        state[c, "b2"] = send(i + 1, t2.at[c, 1, pl.ds((1 - p) * 2, 2)], l2.at[c, 1], dev_a)

    def halve3(c):
        i = c * PER_CHUNK + 4
        state[c, "a2"].wait_recv()
        state[c, "b2"].wait_recv()
        t3[c, 1, 0] = t2[c, 0, q * 2 + 1 - xh] + l2[c, 0, 1 - xh]
        t3[c, 1, 1] = t2[c, 1, p * 2 + 1 - xh] + l2[c, 1, 1 - xh]
        state[c, "x3"] = send(i, t3.at[c, 1], l3.at[c], dev_x)
        t3[c, 0, 0] = t2[c, 0, q * 2 + xh] + l2[c, 0, xh]
        t3[c, 0, 1] = t2[c, 1, p * 2 + xh] + l2[c, 1, xh]

    mine = core * 16

    def blocks(c, at, n):
        return proj.at[c, pl.ds(at, n)]

    def share(c):
        i = c * PER_CHUNK + 5
        state[c, "x3"].wait_recv()
        done = (t3[c, 0] + l3[c]).astype(BF16)
        at_a = mine + p * 4 + q * 2 + xh
        at_b = mine + 8 + q * 4 + p * 2 + xh
        proj[c, at_a] = done[0]
        proj[c, at_b] = done[1]
        state[c, "xa"] = send(i, blocks(c, at_a, 1), blocks(c, at_a, 1), dev_x)
        state[c, "xb"] = send(i + 1, blocks(c, at_b, 1), blocks(c, at_b, 1), dev_x)

    def spread2(c):
        i = c * PER_CHUNK + 7
        state[c, "xa"].wait_recv()
        state[c, "xb"].wait_recv()
        a = blocks(c, mine + p * 4 + q * 2, 2)
        b = blocks(c, mine + 8 + q * 4 + p * 2, 2)
        state[c, "ga2"] = send(i, a, a, dev_b)
        state[c, "gb2"] = send(i + 1, b, b, dev_a)
        state[c, "sib"] = [send(i + 2, a, a, sib), send(i + 3, b, b, sib)]

    def spread4(c):
        i = c * PER_CHUNK + 11
        state[c, "ga2"].wait_recv()
        state[c, "gb2"].wait_recv()
        a = blocks(c, mine + p * 4, 4)
        b = blocks(c, mine + 8 + q * 4, 4)
        state[c, "ga4"] = send(i, a, a, dev_a)
        state[c, "gb4"] = send(i + 1, b, b, dev_b)
        a = blocks(c, mine + p * 4 + (1 - q) * 2, 2)
        b = blocks(c, mine + 8 + q * 4 + (1 - p) * 2, 2)
        state[c, "sib"] += [send(i + 2, a, a, sib), send(i + 3, b, b, sib)]

    def spread_core(c):
        i = c * PER_CHUNK + 15
        state[c, "ga4"].wait_recv()
        state[c, "gb4"].wait_recv()
        a = blocks(c, mine + (1 - p) * 4, 4)
        b = blocks(c, mine + 8 + (1 - q) * 4, 4)
        state[c, "sib"] += [send(i, a, a, sib), send(i + 1, b, b, sib)]

    def local_update(c):
        for copy in state[c, "sib"]:
            copy.wait_recv()
        pc = proj[c].reshape(1024, cw)
        projt[c * cw:(c + 1) * cw, :] = pc.T
        gram = dot(projt[0:(c + 1) * cw, :], pc)
        j = lax.broadcasted_iota(jnp.int32, gram.shape, 0)
        k = lax.broadcasted_iota(jnp.int32, gram.shape, 1) + c * cw
        upper = jnp.where(j <= k, gram, 0.0)
        high = upper.astype(BF16)
        low = (upper - high.astype(F32)).astype(BF16)
        rows = vv[:, 0:(c + 1) * cw]
        total = (dot(ft[...], pc) - (dot(rows, high) + dot(rows, low))) * scale
        wf[c] = total.reshape(8, 2, BLK, cw)
        i = c * PER_CHUNK + 17
        far = (z + 4) % 8
        hop1[c] = wf[c, far].astype(BF16)
        state[c, "u1"] = send(i, hop1.at[c, 0], hop1r.at[c, 0], up)
        state[c, "d1"] = send(i + 1, hop1.at[c, 1], hop1r.at[c, 1], down)

    def chain2(c):
        i = c * PER_CHUNK + 19
        state[c, "u1"].wait_recv()
        at = (z + 3) % 8
        hop2[c, 0, 0, 0] = (wf[c, at, 0] + hop1r[c, 0].astype(F32)).astype(BF16)
        hop2[c, 0, 0, 1] = wf[c, at, 1].astype(BF16)
        state[c, "u2"] = send(i, hop2.at[c, 0, 0], hop2r.at[c, 0, 0], up)
        state[c, "d1"].wait_recv()
        at = (z + 5) % 8
        hop2[c, 0, 1, 0] = wf[c, at, 0].astype(BF16)
        hop2[c, 0, 1, 1] = (wf[c, at, 1] + hop1r[c, 1].astype(F32)).astype(BF16)
        state[c, "d2"] = send(i + 1, hop2.at[c, 0, 1], hop2r.at[c, 0, 1], down)

    def chain3(c):
        i = c * PER_CHUNK + 21
        state[c, "u2"].wait_recv()
        hop2[c, 1, 0] = (wf[c, (z + 2) % 8] + hop2r[c, 0, 0].astype(F32)).astype(BF16)
        state[c, "u3"] = send(i, hop2.at[c, 1, 0], hop2r.at[c, 1, 0], up)
        state[c, "d2"].wait_recv()
        hop2[c, 1, 1] = (wf[c, (z + 6) % 8] + hop2r[c, 0, 1].astype(F32)).astype(BF16)
        state[c, "d3"] = send(i + 1, hop2.at[c, 1, 1], hop2r.at[c, 1, 1], down)

    def chain4(c):
        i = c * PER_CHUNK + 23
        state[c, "u3"].wait_recv()
        hop4[c, 0] = wf[c, (z + 1) % 8] + hop2r[c, 1, 0].astype(F32)
        state[c, "u4"] = send(i, hop4.at[c, 0], hop4r.at[c, 0], up)
        state[c, "d3"].wait_recv()
        hop4[c, 1] = wf[c, (z + 7) % 8] + hop2r[c, 1, 1].astype(F32)
        state[c, "d4"] = send(i + 1, hop4.at[c, 1], hop4r.at[c, 1], down)

    def chain_x(c):
        i = c * PER_CHUNK + 25
        state[c, "u4"].wait_recv()
        state[c, "d4"].wait_recv()
        xs[c, 0] = wf[c, z, 1 - xl] + hop4r[c, 0, 1 - xl] + hop4r[c, 1, 1 - xl]
        state[c, "xl"] = send(i, xs.at[c, 0], xr.at[c], dev_l)
        xs[c, 1] = wf[c, z, xl] + hop4r[c, 0, xl] + hop4r[c, 1, xl]

    def finish(c):
        i = c * PER_CHUNK + 26
        state[c, "xl"].wait_recv()
        at = z * 2 + xl
        ob[c, at] = (xs[c, 1] + xr[c]).astype(BF16)
        state[c, "o0"] = send(i, ob.at[c, at], ob.at[c, at], dev_l)

    def ring(c, hop, at_up, at_down, n):
        i = c * PER_CHUNK + 27 + 2 * hop
        a, b = ob.at[c, pl.ds(at_up, n)], ob.at[c, pl.ds(at_down, n)]
        state[c, "up", hop] = send(i, a, a, up)
        state[c, "down", hop] = send(i + 1, b, b, down)

    def ring_wait(c, hop):
        state[c, "up", hop].wait_recv()
        state[c, "down", hop].wait_recv()

    def ring1(c):
        state[c, "o0"].wait_recv()
        ring(c, 0, z * 2, z * 2, 2)

    def ring2(c):
        ring_wait(c, 0)
        ring(c, 1, ((z + 7) % 8) * 2, ((z + 1) % 8) * 2, 2)

    def ring3(c):
        ring_wait(c, 1)
        ring(c, 2, ((z + 6) % 8) * 2, ((z + 2) % 8) * 2, 2)

    def ring4(c):
        ring_wait(c, 2)
        ring(c, 3, ((z + 5) % 8) * 2, ((z + 3) % 8) * 2 + 1, 1)

    def write(c):
        ring_wait(c, 3)
        copy = pltpu.make_async_copy(ob.at[c], out_hbm.at[:, :, c * cw:(c + 1) * cw], local_sem.at[2 + c])
        copy.start()
        state[c, "out"] = copy

    stages = [project, halve2, halve3, share, spread2, spread4, spread_core, local_update, chain2, chain3,
              chain4, chain_x, finish, ring1, ring2, ring3, ring4, write]
    for tick in range(len(stages) + SKEW * (CHUNKS - 1)):
        for c in range(CHUNKS):
            at = tick - SKEW * c
            if 0 <= at < len(stages):
                stages[at](c)
    for copy in sent:
        copy.wait_send()
    for c in range(CHUNKS):
        state[c, "out"].wait()


def body(features, panel):
    rows, width = features.shape
    k = panel.shape[1]
    cw = k // CHUNKS
    n = CHUNKS
    scale = math.sqrt(D) / (rows * lax.axis_size("sample"))
    scratch = [
        pltpu.VMEM((rows, width), BF16),
        pltpu.VMEM((width, rows), BF16),
        pltpu.VMEM((rows // 2, width), BF16),
        pltpu.VMEM((width, k), BF16),
        pltpu.VMEM((n, width, cw), BF16),
        pltpu.VMEM((n, 16, BLK, cw), F32),
        pltpu.VMEM((n, 2, 4, BLK, cw), F32),
        pltpu.VMEM((n, 2, 4, BLK, cw), F32),
        pltpu.VMEM((n, 2, 2, BLK, cw), F32),
        pltpu.VMEM((n, 2, 2, BLK, cw), F32),
        pltpu.VMEM((n, 2, BLK, cw), F32),
        pltpu.VMEM((n, 32, BLK, cw), BF16),
        pltpu.VMEM((k, rows), BF16),
        pltpu.VMEM((n, 8, 2, BLK, cw), F32),
        pltpu.VMEM((n, 2, BLK, cw), BF16),
        pltpu.VMEM((n, 2, BLK, cw), BF16),
        pltpu.VMEM((n, 2, 2, 2, BLK, cw), BF16),
        pltpu.VMEM((n, 2, 2, 2, BLK, cw), BF16),
        pltpu.VMEM((n, 2, 2, BLK, cw), F32),
        pltpu.VMEM((n, 2, 2, BLK, cw), F32),
        pltpu.VMEM((n, 2, BLK, cw), F32),
        pltpu.VMEM((n, BLK, cw), F32),
        pltpu.VMEM((n, 16, BLK, cw), BF16),
        pltpu.SemaphoreType.DMA((n * PER_CHUNK + 1 + n,)),
        pltpu.SemaphoreType.DMA((n * PER_CHUNK + 1 + n,)),
        pltpu.SemaphoreType.DMA((2 + n,)),
    ]
    out = pl.pallas_call(
        lambda *refs: kernel(scale, *refs),
        out_shape=jax.ShapeDtypeStruct((16, BLK, k), BF16),
        in_specs=[pl.BlockSpec(memory_space=pl.ANY)] * 2,
        out_specs=pl.BlockSpec(memory_space=pl.ANY),
        scratch_shapes=scratch,
        compiler_params=pltpu.CompilerParams(
            collective_id=0, has_side_effects=True, vmem_limit_bytes=60 * 2**20
        ),
        cost_estimate=pl.CostEstimate(flops=6 * 10**9, bytes_accessed=4 * 2**20, transcendentals=0),
        name="update",
    )(features, panel)
    return out.reshape(width, k).astype(F32)


def solution(mesh):
    return jax.shard_map(
        body,
        mesh=mesh,
        in_specs=(P("sample", "feat"), P("feat", None)),
        out_specs=P("feat", None),
        check_vma=False,
    )
```

```python
import math

import jax
import jax.numpy as jnp
from jax import lax
from jax.experimental import pallas as pl
from jax.experimental.pallas import tpu as pltpu
from jax.sharding import PartitionSpec as P

MESH = pl.DeviceIdType.MESH
F32, BF16 = jnp.float32, jnp.bfloat16
D = 8192
CHUNKS = 4
PER_CHUNK = 45
ORDER = (
    0, 1, 2, 3, 0, 1, 2, 3, 0, 1, 2, 3, 0, 1, 2, 0, 3, 0, 1, 2, 1, 2,
    3, 0, 3, 1, 2, 0, 3, 1, 2, 0, 3, 1, 2, 0, 3, 1, 2, 0, 3, 1, 2, 3,
)
BLK = 32


def dot(a, b):
    return jnp.dot(a, b, preferred_element_type=F32)


def kernel(scale, f_hbm, v_hbm, out_hbm, fv, ft, fx, vv, vx, psum, l1, t2, l2, proj, projt, wf,
           half_out, half_in, zs_out, zs_in, ob, send_sem, recv_sem, local_sem):
    s, f = lax.axis_index("sample"), lax.axis_index("feat")
    xl, z = s // 8, s % 8
    xh, y, core = f // 8, (f // 2) % 4, f % 2
    q = y // 2
    p = (y + q) % 2
    half = fv.shape[0] // 2
    width = fv.shape[1]
    cw = vv.shape[1] // CHUNKS

    def feat_dev(xh_, y_, core_):
        return (s, xh_ * 8 + y_ * 2 + core_)

    def sample_dev(xl_, z_):
        return (xl_ * 8 + z_, f)

    y_a = y + 1 - 2 * (y % 2)
    y_b = 3 - y
    sib = feat_dev(xh, y, 1 - core)
    dev_a, dev_b = feat_dev(xh, y_a, core), feat_dev(xh, y_b, core)
    dev_x = feat_dev(1 - xh, y, core)
    dev_l = sample_dev(1 - xl, z)
    dev_ax, dev_bx = feat_dev(1 - xh, y_a, core), feat_dev(1 - xh, y_b, core)
    ring = {k: sample_dev(xl, (z + k) % 8) for k in range(1, 8)}

    loads = []
    loads.append(pltpu.make_async_copy(f_hbm, fv, local_sem.at[0]))
    loads.append(pltpu.make_async_copy(v_hbm, vv, local_sem.at[1]))
    for load in loads:
        load.start()

    barrier = pltpu.get_barrier_semaphore()
    for partner in (sib, dev_a, dev_b, dev_x, dev_ax, dev_bx, dev_l, *ring.values()):
        pl.semaphore_signal(barrier, inc=1, device_id=partner, device_id_type=MESH)
    pl.semaphore_wait(barrier, 14)

    sent = []

    def send(index, src, dst, device):
        copy = pltpu.make_async_remote_copy(
            src_ref=src, dst_ref=dst, send_sem=send_sem.at[index], recv_sem=recv_sem.at[index],
            device_id=device, device_id_type=MESH,
        )
        copy.start()
        sent.append(copy)
        return copy

    base = CHUNKS * PER_CHUNK
    got_f = send(base, f_hbm.at[pl.ds(pl.multiple_of((1 - core) * half, half), half), :], fx, sib)
    got_v = [
        send(base + 1 + c, v_hbm.at[:, c * cw:(c + 1) * cw], vx.at[c], sib) for c in range(CHUNKS)
    ]
    state = {}

    def project(c):
        if c == 0:
            for load in loads:
                load.wait()
            got_f.wait_recv()
        got_v[c].wait_recv()
        own = fv[pl.ds(pl.multiple_of(core * half, half), half), :]
        total = dot(own, vv[:, c * cw:(c + 1) * cw]) + dot(fx[...], vx[c])
        psum[c] = total.reshape(16, BLK, cw)
        i = c * PER_CHUNK
        state[c, "a1"] = send(i, psum.at[c, pl.ds((1 - p) * 4, 4)], l1.at[c, 0], dev_a)
        state[c, "b1"] = send(i + 1, psum.at[c, pl.ds(8 + (1 - q) * 4, 4)], l1.at[c, 1], dev_b)
        if c == 0:
            ft[...] = fv[...].T

    def halve2(c):
        i = c * PER_CHUNK + 2
        state[c, "a1"].wait_recv()
        t2[c, 0] = psum[c, pl.ds(p * 4, 4)] + l1[c, 0]
        at, flip = (q * 2, (1 - q) * 2)
        state[c, "r2"] = [
            send(i, t2.at[c, 0, flip + 1 - xh], l2.at[c, 0, 0], dev_bx),
            send(i + 1, t2.at[c, 0, at + 1 - xh], l2.at[c, 0, 1], dev_x),
            send(i + 2, t2.at[c, 0, flip + xh], l2.at[c, 0, 2], dev_b),
        ]
        state[c, "b1"].wait_recv()
        t2[c, 1] = psum[c, pl.ds(8 + q * 4, 4)] + l1[c, 1]
        at, flip = (p * 2, (1 - p) * 2)
        state[c, "r2"] += [
            send(i + 3, t2.at[c, 1, flip + 1 - xh], l2.at[c, 1, 0], dev_ax),
            send(i + 4, t2.at[c, 1, at + 1 - xh], l2.at[c, 1, 1], dev_x),
            send(i + 5, t2.at[c, 1, flip + xh], l2.at[c, 1, 2], dev_a),
        ]

    mine = core * 16

    def blocks(c, at, n):
        return proj.at[c, pl.ds(at, n)]

    def share(c):
        i = c * PER_CHUNK + 8
        for copy in state[c, "r2"]:
            copy.wait_recv()
        at_a = mine + p * 4 + q * 2 + xh
        at_b = mine + 8 + q * 4 + p * 2 + xh
        proj[c, at_a] = (t2[c, 0, q * 2 + xh] + l2[c, 0, 0] + l2[c, 0, 1] + l2[c, 0, 2]).astype(BF16)
        a = proj.at[c, at_a]
        state[c, "g2"] = [send(i, a, a, dev_bx), send(i + 1, a, a, dev_x), send(i + 2, a, a, dev_b)]
        proj[c, at_b] = (t2[c, 1, p * 2 + xh] + l2[c, 1, 0] + l2[c, 1, 1] + l2[c, 1, 2]).astype(BF16)
        b = proj.at[c, at_b]
        state[c, "g2"] += [send(i + 3, b, b, dev_ax), send(i + 4, b, b, dev_x), send(i + 5, b, b, dev_a)]

    def spread4(c):
        i = c * PER_CHUNK + 14
        for copy in state[c, "g2"]:
            copy.wait_recv()
        a = blocks(c, mine + p * 4, 4)
        b = blocks(c, mine + 8 + q * 4, 4)
        state[c, "ga4"] = send(i, a, a, dev_a)
        state[c, "gb4"] = send(i + 1, b, b, dev_b)
        state[c, "sib"] = [send(i + 2, a, a, sib), send(i + 3, b, b, sib)]

    def spread_core(c):
        i = c * PER_CHUNK + 18
        state[c, "ga4"].wait_recv()
        state[c, "gb4"].wait_recv()
        a = blocks(c, mine + (1 - p) * 4, 4)
        b = blocks(c, mine + 8 + (1 - q) * 4, 4)
        state[c, "sib"] += [send(i, a, a, sib), send(i + 1, b, b, sib)]

    def local_update(c):
        for copy in state[c, "sib"]:
            copy.wait_recv()
        pc = proj[c].reshape(1024, cw)
        projt[c * cw:(c + 1) * cw, :] = pc.T
        gram = dot(projt[0:(c + 1) * cw, :], pc)
        j = lax.broadcasted_iota(jnp.int32, gram.shape, 0)
        k = lax.broadcasted_iota(jnp.int32, gram.shape, 1) + c * cw
        upper = jnp.where(j <= k, gram, 0.0)
        high = upper.astype(BF16)
        low = (upper - high.astype(F32)).astype(BF16)
        rows = vv[:, 0:(c + 1) * cw]
        total = (dot(ft[...], pc) - (dot(rows, high) + dot(rows, low))) * scale
        wf[c] = total.reshape(2, 8, BLK, cw)
        half_out[c] = wf[c, 1 - xl].astype(BF16)
        state[c, "xl"] = send(c * PER_CHUNK + 20, half_out.at[c], half_in.at[c], dev_l)

    def scatter(c):
        i = c * PER_CHUNK + 21
        state[c, "xl"].wait_recv()
        both = wf[c, xl] + half_in[c].astype(F32)
        wf[c, xl] = both
        zs_out[c] = both.astype(BF16)
        state[c, "zs"] = [
            send(i + k, zs_out.at[c, (z + k) % 8], zs_in.at[c, k - 1], ring[k]) for k in (4, 3, 5, 2, 6, 1, 7)
        ]

    def finish(c):
        i = c * PER_CHUNK + 29
        for copy in state[c, "zs"]:
            copy.wait_recv()
        total = wf[c, xl, z]
        for k in range(7):
            total = total + zs_in[c, k].astype(F32)
        at = xl * 8 + z
        ob[c, at] = total.astype(BF16)
        a = ob.at[c, at]
        state[c, "o1"] = [send(i + n, a, a, ring[k]) for n, k in enumerate((2, 6, 1, 7))]
        state[c, "ox"] = [send(i + 4, a, a, dev_l)]

    def own(c, k):
        return ob.at[c, xl * 8 + (z + k) % 8]

    def gather2(c):
        i = c * PER_CHUNK + 34
        up2, down2, up1, down1 = state[c, "o1"]
        down1.wait_recv()
        up2.wait_recv()
        a, b = own(c, 1), own(c, 6)
        state[c, "o2"] = [send(i, a, a, ring[6])]
        b2 = b.at[pl.ds(0, BLK // 2)]
        state[c, "o2"] += [send(i + 1, b2, b2, ring[2])]
        up1.wait_recv()
        down2.wait_recv()
        a, b = own(c, 7), own(c, 2)
        state[c, "o2"] += [send(i + 2, a, a, ring[2])]
        b2 = b.at[pl.ds(BLK // 2, BLK // 2)]
        state[c, "o2"] += [send(i + 3, b2, b2, ring[6])]
        for n, k in enumerate((1, 7, 2, 6)):
            a = own(c, k)
            state[c, "ox"] += [send(i + 4 + n, a, a, dev_l)]

    def swap(c):
        i = c * PER_CHUNK + 42
        for copy in state[c, "o2"]:
            copy.wait_recv()
        for n, k in enumerate((3, 4, 5)):
            a = own(c, k)
            state[c, "ox"] += [send(i + n, a, a, dev_l)]

    def write(c):
        for copy in state[c, "ox"]:
            copy.wait_recv()
        copy = pltpu.make_async_copy(ob.at[c], out_hbm.at[:, :, c * cw:(c + 1) * cw], local_sem.at[2 + c])
        copy.start()
        state[c, "out"] = copy

    stages = [project, halve2, share, spread4, spread_core, local_update, scatter, finish, gather2, swap, write]
    done = [0] * CHUNKS
    for c in ORDER:
        stages[done[c]](c)
        done[c] += 1
    for copy in sent:
        copy.wait_send()
    for c in range(CHUNKS):
        state[c, "out"].wait()


def body(features, panel):
    rows, width = features.shape
    k = panel.shape[1]
    cw = k // CHUNKS
    n = CHUNKS
    scale = math.sqrt(D) / (rows * lax.axis_size("sample"))
    scratch = [
        pltpu.VMEM((rows, width), BF16),
        pltpu.VMEM((width, rows), BF16),
        pltpu.VMEM((rows // 2, width), BF16),
        pltpu.VMEM((width, k), BF16),
        pltpu.VMEM((n, width, cw), BF16),
        pltpu.VMEM((n, 16, BLK, cw), F32),
        pltpu.VMEM((n, 2, 4, BLK, cw), F32),
        pltpu.VMEM((n, 2, 4, BLK, cw), F32),
        pltpu.VMEM((n, 2, 3, BLK, cw), F32),
        pltpu.VMEM((n, 32, BLK, cw), BF16),
        pltpu.VMEM((k, rows), BF16),
        pltpu.VMEM((n, 2, 8, BLK, cw), F32),
        pltpu.VMEM((n, 8, BLK, cw), BF16),
        pltpu.VMEM((n, 8, BLK, cw), BF16),
        pltpu.VMEM((n, 8, BLK, cw), BF16),
        pltpu.VMEM((n, 7, BLK, cw), BF16),
        pltpu.VMEM((n, 16, BLK, cw), BF16),
        pltpu.SemaphoreType.DMA((n * PER_CHUNK + 1 + n,)),
        pltpu.SemaphoreType.DMA((n * PER_CHUNK + 1 + n,)),
        pltpu.SemaphoreType.DMA((2 + n,)),
    ]
    out = pl.pallas_call(
        lambda *refs: kernel(scale, *refs),
        out_shape=jax.ShapeDtypeStruct((16, BLK, k), BF16),
        in_specs=[pl.BlockSpec(memory_space=pl.ANY)] * 2,
        out_specs=pl.BlockSpec(memory_space=pl.ANY),
        scratch_shapes=scratch,
        compiler_params=pltpu.CompilerParams(
            collective_id=0, has_side_effects=True, vmem_limit_bytes=60 * 2**20
        ),
        cost_estimate=pl.CostEstimate(flops=6 * 10**9, bytes_accessed=4 * 2**20, transcendentals=0),
        name="update",
    )(features, panel)
    return out.reshape(width, k).astype(F32)


def solution(mesh):
    return jax.shard_map(
        body,
        mesh=mesh,
        in_specs=(P("sample", "feat"), P("feat", None)),
        out_specs=P("feat", None),
        check_vma=False,
    )
```

```python
import math

import jax
import jax.numpy as jnp
from jax import lax
from jax.experimental import pallas as pl
from jax.experimental.pallas import tpu as pltpu
from jax.sharding import PartitionSpec as P

MESH = pl.DeviceIdType.MESH
F32, BF16 = jnp.float32, jnp.bfloat16
D = 8192
CHUNKS = 4
PER_CHUNK = 45
TURN = 3
ORDER = (
    0, 1, 0, 1, 2, 0, 2, 3, 1, 0, 3, 2, 0, 1, 3, 2, 0, 1, 0, 3, 1, 2, 1, 0,
    2, 3, 2, 3, 1, 0, 3, 2, 0, 3, 1, 2, 0, 3, 0, 1, 2, 3, 1, 2, 3, 1, 2, 3,
)
BLK = 32


def dot(a, b):
    return jnp.dot(a, b, preferred_element_type=F32)


def kernel(scale, f_hbm, v_hbm, out_hbm, fv, ft, vv, part, part_in, psum, l1, t2, l2, proj, projt, wf,
           half_out, half_in, zs_out, zs_in, ob, send_sem, recv_sem, local_sem):
    s, f = lax.axis_index("sample"), lax.axis_index("feat")
    xl, z = s // 8, s % 8
    xh, y, core = f // 8, (f // 2) % 4, f % 2
    q = y // 2
    p = (y + q) % 2
    half = fv.shape[1] // 2
    cw = vv.shape[1] // CHUNKS

    def feat_dev(xh_, y_, core_):
        return (s, xh_ * 8 + y_ * 2 + core_)

    def sample_dev(xl_, z_):
        return (xl_ * 8 + z_, f)

    y_a = y + 1 - 2 * (y % 2)
    y_b = 3 - y
    sib = feat_dev(xh, y, 1 - core)
    dev_a, dev_b = feat_dev(xh, y_a, core), feat_dev(xh, y_b, core)
    dev_x = feat_dev(1 - xh, y, core)
    dev_l = sample_dev(1 - xl, z)
    dev_ax, dev_bx = feat_dev(1 - xh, y_a, core), feat_dev(1 - xh, y_b, core)
    ring = {k: sample_dev(xl, (z + k) % 8) for k in range(1, 8)}

    loads = [pltpu.make_async_copy(v_hbm, vv, local_sem.at[0]), pltpu.make_async_copy(f_hbm, fv, local_sem.at[1])]
    for load in loads:
        load.start()

    barrier = pltpu.get_barrier_semaphore()
    for partner in (sib, dev_a, dev_b, dev_x, dev_ax, dev_bx, dev_l, *ring.values()):
        pl.semaphore_signal(barrier, inc=1, device_id=partner, device_id_type=MESH)
    for load in loads:
        load.wait()

    def partial(c, side):
        rows = fv[pl.ds(pl.multiple_of(side * BLK * 16, BLK * 16), BLK * 16), :]
        return dot(rows, vv[:, c * cw:(c + 1) * cw]).reshape(16, BLK, cw)

    pl.semaphore_wait(barrier, 14)

    sent = []

    def send(index, src, dst, device):
        copy = pltpu.make_async_remote_copy(
            src_ref=src, dst_ref=dst, send_sem=send_sem.at[index], recv_sem=recv_sem.at[index],
            device_id=device, device_id_type=MESH,
        )
        copy.start()
        sent.append(copy)
        return copy

    state = {}

    def project(c):
        part[c] = partial(c, 1 - core)
        state[c, "half"] = send(c * PER_CHUNK, part.at[c], part_in.at[c], sib)
        psum[c] = partial(c, core)

    def fold(c):
        i = c * PER_CHUNK + 1
        state[c, "half"].wait_recv()
        at = pl.ds((1 - p) * 4, 4)
        psum[c, at] = psum[c, at] + part_in[c, at]
        state[c, "a1"] = send(i, psum.at[c, at], l1.at[c, 0], dev_a)
        at = pl.ds(8 + (1 - q) * 4, 4)
        psum[c, at] = psum[c, at] + part_in[c, at]
        state[c, "b1"] = send(i + 1, psum.at[c, at], l1.at[c, 1], dev_b)
        for at in (pl.ds(p * 4, 4), pl.ds(8 + q * 4, 4)):
            psum[c, at] = psum[c, at] + part_in[c, at]
        if c == TURN:
            ft[...] = fv[...].T

    def halve2(c):
        i = c * PER_CHUNK + 3
        state[c, "a1"].wait_recv()
        for slot, at in enumerate((q * 2 + 1 - xh, (1 - q) * 2 + 1 - xh, (1 - q) * 2 + xh, q * 2 + xh)):
            t2[c, 2 * slot] = psum[c, p * 4 + at] + l1[c, 0, at]
        copies = [
            send(i, t2.at[c, 2], l2.at[c, 2], dev_bx),
            send(i + 1, t2.at[c, 4], l2.at[c, 4], dev_b),
        ]
        state[c, "b1"].wait_recv()
        for slot, at in enumerate((p * 2 + 1 - xh, (1 - p) * 2 + 1 - xh, (1 - p) * 2 + xh, p * 2 + xh)):
            t2[c, 2 * slot + 1] = psum[c, 8 + q * 4 + at] + l1[c, 1, at]
        copies += [
            send(i + 2, t2.at[c, 3], l2.at[c, 3], dev_ax),
            send(i + 3, t2.at[c, pl.ds(0, 2)], l2.at[c, pl.ds(0, 2)], dev_x),
            send(i + 4, t2.at[c, 5], l2.at[c, 5], dev_a),
        ]
        state[c, "r2"] = copies

    def share(c):
        i = c * PER_CHUNK + 8
        for copy in state[c, "r2"]:
            copy.wait_recv()
        total = (t2[c, 6:8] + l2[c, 0:2] + l2[c, 2:4] + l2[c, 4:6]).astype(BF16)
        at_a = p * 4 + q * 2 + xh
        at_b = 8 + q * 4 + p * 2 + xh
        proj[c, core, at_a] = total[0]
        proj[c, core, at_b] = total[1]
        a, b = proj.at[c, core, at_a], proj.at[c, core, at_b]
        state[c, "g2"] = [
            send(i, a, a, dev_bx),
            send(i + 1, b, b, dev_ax),
            send(i + 2, a, a, dev_x),
            send(i + 3, b, b, dev_x),
            send(i + 4, a, a, dev_b),
            send(i + 5, b, b, dev_a),
        ]

    def spread4(c):
        i = c * PER_CHUNK + 14
        for copy in state[c, "g2"]:
            copy.wait_recv()
        a = proj.at[c, core, pl.ds(p * 4, 4)]
        b = proj.at[c, core, pl.ds(8 + q * 4, 4)]
        state[c, "g4"] = [send(i, a, a, dev_a), send(i + 1, b, b, dev_b)]

    def spread_core(c):
        for copy in state[c, "g4"]:
            copy.wait_recv()
        a = proj.at[c, core]
        state[c, "sib"] = send(c * PER_CHUNK + 16, a, a, sib)

    def local_update(c):
        state[c, "sib"].wait_recv()
        pc = proj[c].reshape(1024, cw)
        projt[c * cw:(c + 1) * cw, :] = pc.T
        gram = dot(projt[0:(c + 1) * cw, :], pc)
        j = lax.broadcasted_iota(jnp.int32, gram.shape, 0)
        k = lax.broadcasted_iota(jnp.int32, gram.shape, 1) + c * cw
        upper = jnp.where(j <= k, gram, 0.0)
        high = upper.astype(BF16)
        low = (upper - high.astype(F32)).astype(BF16)

        def rows_of(side):
            at = pl.ds(pl.multiple_of(side * half, half), half)
            rows = vv[at, 0:(c + 1) * cw]
            total = (dot(ft[at, :], pc) - (dot(rows, high) + dot(rows, low))) * scale
            return total.reshape(8, BLK, cw)

        half_out[c] = rows_of(1 - xl).astype(BF16)
        state[c, "xl"] = send(c * PER_CHUNK + 20, half_out.at[c], half_in.at[c], dev_l)
        wf[c] = rows_of(xl)

    def scatter(c):
        i = c * PER_CHUNK + 21
        state[c, "xl"].wait_recv()
        both = wf[c] + half_in[c].astype(F32)
        wf[c] = both
        zs_out[c] = both.astype(BF16)
        state[c, "zs"] = [
            send(i + k, zs_out.at[c, (z + k) % 8], zs_in.at[c, k - 1], ring[k]) for k in (4, 3, 5, 2, 6, 1, 7)
        ]

    def finish(c):
        i = c * PER_CHUNK + 29
        for copy in state[c, "zs"]:
            copy.wait_recv()
        total = wf[c, z]
        for k in range(7):
            total = total + zs_in[c, k].astype(F32)
        at = xl * 8 + z
        ob[c, at] = total.astype(BF16)
        a = ob.at[c, at]
        state[c, "o1"] = [send(i + n, a, a, ring[k]) for n, k in enumerate((2, 6, 1, 7))]
        state[c, "ox"] = [send(i + 4, a, a, dev_l)]

    def own(c, k):
        return ob.at[c, xl * 8 + (z + k) % 8]

    def gather2(c):
        i = c * PER_CHUNK + 34
        up2, down2, up1, down1 = state[c, "o1"]
        down1.wait_recv()
        up2.wait_recv()
        a, b = own(c, 1), own(c, 6)
        state[c, "o2"] = [send(i, a, a, ring[6])]
        b2 = b.at[pl.ds(0, BLK // 2)]
        state[c, "o2"] += [send(i + 1, b2, b2, ring[2])]
        up1.wait_recv()
        down2.wait_recv()
        a, b = own(c, 7), own(c, 2)
        state[c, "o2"] += [send(i + 2, a, a, ring[2])]
        b2 = b.at[pl.ds(BLK // 2, BLK // 2)]
        state[c, "o2"] += [send(i + 3, b2, b2, ring[6])]
        for n, k in enumerate((1, 7, 2, 6)):
            a = own(c, k)
            state[c, "ox"] += [send(i + 4 + n, a, a, dev_l)]

    def swap(c):
        i = c * PER_CHUNK + 42
        for copy in state[c, "o2"]:
            copy.wait_recv()
        for n, k in enumerate((3, 4, 5)):
            a = own(c, k)
            state[c, "ox"] += [send(i + n, a, a, dev_l)]

    def write(c):
        for copy in state[c, "ox"]:
            copy.wait_recv()
        copy = pltpu.make_async_copy(ob.at[c], out_hbm.at[:, :, c * cw:(c + 1) * cw], local_sem.at[2 + c])
        copy.start()
        state[c, "out"] = copy

    stages = [project, fold, halve2, share, spread4, spread_core, local_update, scatter, finish, gather2, swap, write]
    done = [0] * CHUNKS
    for c in ORDER:
        stages[done[c]](c)
        done[c] += 1
    for copy in sent:
        copy.wait_send()
    for c in range(CHUNKS):
        state[c, "out"].wait()


def body(features, panel):
    rows, width = features.shape
    k = panel.shape[1]
    cw = k // CHUNKS
    n = CHUNKS
    scale = math.sqrt(D) / (rows * lax.axis_size("sample"))
    scratch = [
        pltpu.VMEM((rows, width), BF16),
        pltpu.VMEM((width, rows), BF16),
        pltpu.VMEM((width, k), BF16),
        pltpu.VMEM((n, 16, BLK, cw), F32),
        pltpu.VMEM((n, 16, BLK, cw), F32),
        pltpu.VMEM((n, 16, BLK, cw), F32),
        pltpu.VMEM((n, 2, 4, BLK, cw), F32),
        pltpu.VMEM((n, 8, BLK, cw), F32),
        pltpu.VMEM((n, 6, BLK, cw), F32),
        pltpu.VMEM((n, 2, 16, BLK, cw), BF16),
        pltpu.VMEM((k, rows), BF16),
        pltpu.VMEM((n, 8, BLK, cw), F32),
        pltpu.VMEM((n, 8, BLK, cw), BF16),
        pltpu.VMEM((n, 8, BLK, cw), BF16),
        pltpu.VMEM((n, 8, BLK, cw), BF16),
        pltpu.VMEM((n, 7, BLK, cw), BF16),
        pltpu.VMEM((n, 16, BLK, cw), BF16),
        pltpu.SemaphoreType.DMA((n * PER_CHUNK,)),
        pltpu.SemaphoreType.DMA((n * PER_CHUNK,)),
        pltpu.SemaphoreType.DMA((2 + n,)),
    ]
    out = pl.pallas_call(
        lambda *refs: kernel(scale, *refs),
        out_shape=jax.ShapeDtypeStruct((16, BLK, k), BF16),
        in_specs=[pl.BlockSpec(memory_space=pl.ANY)] * 2,
        out_specs=pl.BlockSpec(memory_space=pl.ANY),
        scratch_shapes=scratch,
        compiler_params=pltpu.CompilerParams(
            collective_id=0, has_side_effects=True, vmem_limit_bytes=60 * 2**20
        ),
        cost_estimate=pl.CostEstimate(flops=6 * 10**9, bytes_accessed=4 * 2**20, transcendentals=0),
        name="update",
    )(features, panel)
    return out.reshape(width, k).astype(F32)


def solution(mesh):
    return jax.shard_map(
        body,
        mesh=mesh,
        in_specs=(P("sample", "feat"), P("feat", None)),
        out_specs=P("feat", None),
        check_vma=False,
    )
```

```python
import math

import jax
import jax.numpy as jnp
from jax import lax
from jax.experimental import pallas as pl
from jax.experimental.pallas import tpu as pltpu
from jax.sharding import PartitionSpec as P

MESH = pl.DeviceIdType.MESH
F32, BF16 = jnp.float32, jnp.bfloat16
D = 8192
WIDTHS = (128, 256, 256, 256, 128)
CHUNKS = len(WIDTHS)
START = tuple(sum(WIDTHS[:c]) for c in range(CHUNKS + 1))
PER_CHUNK = 45
TURN = 4
PIECES = 2
ORDER = (0, 1, 0, 1, 2, 0, 2, 3, 1, 4, 0, 3, 2, 1, 0, 3, 4, 1, 0, 2, 0, 4, 3, 1, 2, 1, 0, 2, 3, 4, 2, 3, 0, 1, 4, 3, 0, 2, 4, 1, 4, 3, 4, 0, 1, 3, 2, 4, 1, 3, 2, 0, 4, 1, 3, 2, 4, 3, 2, 4)
BLK = 32
LAST = -1
NEAR = (1, 7, 2, 6, 3, 5, 4)


def dot(a, b):
    return jnp.dot(a, b, preferred_element_type=F32)


def kernel(scale, f_hbm, v_hbm, out_hbm, fv, ft, vv, part, part_in, psum, l1, t2, l2, proj, projt, wf,
           half_out, half_in, zs_out, zs_in, ob, send_sem, recv_sem, local_sem):
    s, f = lax.axis_index("sample"), lax.axis_index("feat")
    xl, z = s // 8, s % 8
    xh, y, core = f // 8, (f // 2) % 4, f % 2
    q = y // 2
    p = (y + q) % 2
    half = fv.shape[1] // 2

    def feat_dev(xh_, y_, core_):
        return (s, xh_ * 8 + y_ * 2 + core_)

    def sample_dev(xl_, z_):
        return (xl_ * 8 + z_, f)

    y_a = y + 1 - 2 * (y % 2)
    y_b = 3 - y
    sib = feat_dev(xh, y, 1 - core)
    dev_a, dev_b = feat_dev(xh, y_a, core), feat_dev(xh, y_b, core)
    dev_x = feat_dev(1 - xh, y, core)
    dev_l = sample_dev(1 - xl, z)
    dev_ax, dev_bx = feat_dev(1 - xh, y_a, core), feat_dev(1 - xh, y_b, core)
    ring = {k: sample_dev(xl, (z + k) % 8) for k in range(1, 8)}

    loads = [pltpu.make_async_copy(v_hbm, vv, local_sem.at[0]), pltpu.make_async_copy(f_hbm, fv, local_sem.at[1])]
    for load in loads:
        load.start()

    barrier = pltpu.get_barrier_semaphore()
    for partner in (sib, dev_a, dev_b, dev_x, dev_ax, dev_bx, dev_l, *ring.values()):
        pl.semaphore_signal(barrier, inc=1, device_id=partner, device_id_type=MESH)
    for load in loads:
        load.wait()

    def partial(c, side):
        rows = fv[pl.ds(pl.multiple_of(side * BLK * 16, BLK * 16), BLK * 16), :]
        return dot(rows, vv[:, START[c]:START[c + 1]]).reshape(16, BLK, WIDTHS[c])

    pl.semaphore_wait(barrier, 14)

    sent = []

    def send(index, src, dst, device):
        copy = pltpu.make_async_remote_copy(
            src_ref=src, dst_ref=dst, send_sem=send_sem.at[index], recv_sem=recv_sem.at[index],
            device_id=device, device_id_type=MESH,
        )
        copy.start()
        sent.append(copy)
        return copy

    state = {}

    def project(c):
        part[c][...] = partial(c, 1 - core)
        state[c, "half"] = send(c * PER_CHUNK, part[c], part_in[c], sib)
        psum[c][...] = partial(c, core)

    def fold(c):
        i = c * PER_CHUNK + 1
        state[c, "half"].wait_recv()
        at = pl.ds((1 - p) * 4, 4)
        psum[c][at] = psum[c][at] + part_in[c][at]
        state[c, "a1"] = send(i, psum[c].at[at], l1[c].at[0], dev_a)
        at = pl.ds(8 + (1 - q) * 4, 4)
        psum[c][at] = psum[c][at] + part_in[c][at]
        state[c, "b1"] = send(i + 1, psum[c].at[at], l1[c].at[1], dev_b)
        for at in (pl.ds(p * 4, 4), pl.ds(8 + q * 4, 4)):
            psum[c][at] = psum[c][at] + part_in[c][at]
        if c == TURN:
            ft[...] = fv[...].T

    def halve2(c):
        i = c * PER_CHUNK + 3
        state[c, "a1"].wait_recv()
        for slot, at in enumerate((q * 2 + 1 - xh, (1 - q) * 2 + 1 - xh, (1 - q) * 2 + xh, q * 2 + xh)):
            t2[c][2 * slot] = psum[c][p * 4 + at] + l1[c][0, at]
        copies = [
            send(i, t2[c].at[2], l2[c].at[2], dev_bx),
            send(i + 1, t2[c].at[4], l2[c].at[4], dev_b),
        ]
        state[c, "b1"].wait_recv()
        for slot, at in enumerate((p * 2 + 1 - xh, (1 - p) * 2 + 1 - xh, (1 - p) * 2 + xh, p * 2 + xh)):
            t2[c][2 * slot + 1] = psum[c][8 + q * 4 + at] + l1[c][1, at]
        copies += [
            send(i + 2, t2[c].at[3], l2[c].at[3], dev_ax),
            send(i + 3, t2[c].at[pl.ds(0, 2)], l2[c].at[pl.ds(0, 2)], dev_x),
            send(i + 4, t2[c].at[5], l2[c].at[5], dev_a),
        ]
        state[c, "r2"] = copies

    def share(c):
        i = c * PER_CHUNK + 8
        for copy in state[c, "r2"]:
            copy.wait_recv()
        total = (t2[c][6:8] + l2[c][0:2] + l2[c][2:4] + l2[c][4:6]).astype(BF16)
        at_a = p * 4 + q * 2 + xh
        at_b = 8 + q * 4 + p * 2 + xh
        proj[c][core, at_a] = total[0]
        proj[c][core, at_b] = total[1]
        a, b = proj[c].at[core, at_a], proj[c].at[core, at_b]
        state[c, "g2"] = [
            send(i, a, a, dev_bx),
            send(i + 1, b, b, dev_ax),
            send(i + 2, a, a, dev_x),
            send(i + 3, b, b, dev_x),
            send(i + 4, a, a, dev_b),
            send(i + 5, b, b, dev_a),
        ]

    def spread4(c):
        i = c * PER_CHUNK + 14
        for copy in state[c, "g2"]:
            copy.wait_recv()
        a = proj[c].at[core, pl.ds(p * 4, 4)]
        b = proj[c].at[core, pl.ds(8 + q * 4, 4)]
        state[c, "g4"] = [send(i, a, a, dev_a), send(i + 1, b, b, dev_b)]

    def spread_core(c):
        for copy in state[c, "g4"]:
            copy.wait_recv()
        a = proj[c].at[core]
        state[c, "sib"] = send(c * PER_CHUNK + 16, a, a, sib)

    def local_update(c):
        state[c, "sib"].wait_recv()
        pc = proj[c][...].reshape(1024, WIDTHS[c])
        projt[START[c]:START[c + 1], :] = pc.T
        gram = dot(projt[0:START[c + 1], :], pc)
        j = lax.broadcasted_iota(jnp.int32, gram.shape, 0)
        k = lax.broadcasted_iota(jnp.int32, gram.shape, 1) + START[c]
        upper = jnp.where(j <= k, gram, 0.0)
        high = upper.astype(BF16)
        low = (upper - high.astype(F32)).astype(BF16)

        def rows_of(side):
            at = pl.ds(pl.multiple_of(side * half, half), half)
            rows = vv[at, 0:START[c + 1]]
            total = (dot(ft[at, :], pc) - (dot(rows, high) + dot(rows, low))) * scale
            return total.reshape(8, BLK, WIDTHS[c])

        half_out[c][...] = rows_of(1 - xl).astype(BF16)
        state[c, "xl"] = send(c * PER_CHUNK + 20, half_out[c], half_in[c], dev_l)
        wf[c][...] = rows_of(xl)

    def scatter(c):
        i = c * PER_CHUNK + 21
        state[c, "xl"].wait_recv()
        both = wf[c][...] + half_in[c][...].astype(F32)
        wf[c][...] = both
        zs_out[c][...] = both.astype(BF16)
        state[c, "zs"] = [
            send(i + k, zs_out[c].at[(z + k) % 8], zs_in[c].at[k - 1], ring[k]) for k in (4, 3, 5, 2, 6, 1, 7)
        ]

    def finish(c):
        i = c * PER_CHUNK + 29
        for copy in state[c, "zs"]:
            copy.wait_recv()
        total = wf[c][z]
        for k in range(7):
            total = total + zs_in[c][k].astype(F32)
        at = xl * 8 + z
        ob[c][at] = total.astype(BF16)
        a = ob[c].at[at]
        if c == LAST:
            state[c, "ox"] = [send(i + 7, a, a, dev_l)]
            state[c, "o1"] = [send(i + n, a, a, ring[k]) for n, k in enumerate(NEAR)]
            return
        state[c, "o1"] = [send(i + n, a, a, ring[k]) for n, k in enumerate((2, 6, 1, 7))]
        state[c, "ox"] = [send(i + 4, a, a, dev_l)]

    def own(c, k):
        return ob[c].at[xl * 8 + (z + k) % 8]

    def relay(c, first, last):
        i = c * PER_CHUNK + 37
        for n in range(first, last):
            state[c, "o1"][n].wait_recv()
            a = own(c, (8 - NEAR[n]) % 8)
            state[c, "ox"] += [send(i + n, a, a, dev_l)]

    def gather2(c):
        if c == LAST:
            return relay(c, 0, 4)
        i = c * PER_CHUNK + 34
        up2, down2, up1, down1 = state[c, "o1"]
        down1.wait_recv()
        up2.wait_recv()
        a, b = own(c, 1), own(c, 6)
        state[c, "o2"] = [send(i, a, a, ring[6])]
        b2 = b.at[pl.ds(0, BLK // 2)]
        state[c, "o2"] += [send(i + 1, b2, b2, ring[2])]
        up1.wait_recv()
        down2.wait_recv()
        a, b = own(c, 7), own(c, 2)
        state[c, "o2"] += [send(i + 2, a, a, ring[2])]
        b2 = b.at[pl.ds(BLK // 2, BLK // 2)]
        state[c, "o2"] += [send(i + 3, b2, b2, ring[6])]
        for n, k in enumerate((1, 7, 2, 6)):
            a = own(c, k)
            state[c, "ox"] += [send(i + 4 + n, a, a, dev_l)]

    def swap(c):
        if c == LAST:
            return relay(c, 4, 7)
        i = c * PER_CHUNK + 42
        for copy in state[c, "o2"]:
            copy.wait_recv()
        for n, k in enumerate((3, 4, 5)):
            a = own(c, k)
            state[c, "ox"] += [send(i + n, a, a, dev_l)]

    def write(c):
        for copy in state[c, "ox"]:
            copy.wait_recv()
        copy = pltpu.make_async_copy(ob[c], out_hbm.at[:, :, START[c]:START[c + 1]], local_sem.at[2 + c])
        copy.start()
        state[c, "out"] = copy

    stages = [project, fold, halve2, share, spread4, spread_core, local_update, scatter, finish, gather2, swap, write]
    done = [0] * CHUNKS
    for c in ORDER:
        stages[done[c]](c)
        done[c] += 1
    for copy in sent:
        copy.wait_send()
    for c in range(CHUNKS):
        state[c, "out"].wait()


def widen_kernel(x_ref, o_ref):
    o_ref[...] = x_ref[...].astype(F32)


def widen(x):
    rows, k = x.shape
    tile = rows // PIECES
    spec = pl.BlockSpec((tile, k), lambda i: (i, 0))
    return pl.pallas_call(
        widen_kernel,
        grid=(PIECES,),
        out_shape=jax.ShapeDtypeStruct((rows, k), F32),
        in_specs=[spec],
        out_specs=spec,
        name="widen",
    )(x)


def body(features, panel):
    rows, width = features.shape
    k = panel.shape[1]
    n = CHUNKS
    scale = math.sqrt(D) / (rows * lax.axis_size("sample"))
    scratch = [
        pltpu.VMEM((rows, width), BF16),
        pltpu.VMEM((width, rows), BF16),
        pltpu.VMEM((width, k), BF16),
        [pltpu.VMEM((16, BLK, w), F32) for w in WIDTHS],
        [pltpu.VMEM((16, BLK, w), F32) for w in WIDTHS],
        [pltpu.VMEM((16, BLK, w), F32) for w in WIDTHS],
        [pltpu.VMEM((2, 4, BLK, w), F32) for w in WIDTHS],
        [pltpu.VMEM((8, BLK, w), F32) for w in WIDTHS],
        [pltpu.VMEM((6, BLK, w), F32) for w in WIDTHS],
        [pltpu.VMEM((2, 16, BLK, w), BF16) for w in WIDTHS],
        pltpu.VMEM((k, rows), BF16),
        [pltpu.VMEM((8, BLK, w), F32) for w in WIDTHS],
        [pltpu.VMEM((8, BLK, w), BF16) for w in WIDTHS],
        [pltpu.VMEM((8, BLK, w), BF16) for w in WIDTHS],
        [pltpu.VMEM((8, BLK, w), BF16) for w in WIDTHS],
        [pltpu.VMEM((7, BLK, w), BF16) for w in WIDTHS],
        [pltpu.VMEM((16, BLK, w), BF16) for w in WIDTHS],
        pltpu.SemaphoreType.DMA((n * PER_CHUNK,)),
        pltpu.SemaphoreType.DMA((n * PER_CHUNK,)),
        pltpu.SemaphoreType.DMA((2 + n,)),
    ]
    out = pl.pallas_call(
        lambda *refs: kernel(scale, *refs),
        out_shape=jax.ShapeDtypeStruct((16, BLK, k), BF16),
        in_specs=[pl.BlockSpec(memory_space=pl.ANY)] * 2,
        out_specs=pl.BlockSpec(memory_space=pl.ANY),
        scratch_shapes=scratch,
        compiler_params=pltpu.CompilerParams(
            collective_id=0, has_side_effects=True, vmem_limit_bytes=60 * 2**20
        ),
        cost_estimate=pl.CostEstimate(flops=6 * 10**9, bytes_accessed=4 * 2**20, transcendentals=0),
        name="update",
    )(features, panel)
    return widen(out.reshape(width, k))


def solution(mesh):
    return jax.shard_map(
        body,
        mesh=mesh,
        in_specs=(P("sample", "feat"), P("feat", None)),
        out_specs=P("feat", None),
        check_vma=False,
    )
```
